32 devices in a mesh: dp: 16 (over z, y, core), tensor: 2 (over x).
Axes of the slice: x: 2, y: 2, z: 4, core: 2. Of those that a mesh axis runs over, the one named last changes fastest.
Arguments:
- tokens: bfloat16 [32768, 1024], P(('dp', 'tensor')), may hold values from -6 to 6
- gain_mix: float32 [1024], replicated, may hold values from 0.5 to 1.5
- proj_in: bfloat16 [1024, 3, 1024], P(None, None, 'tensor'), may hold values from -0.1875 to 0.1875
- conv_filter: float32 [3, 1024], P(None, 'tensor'), may hold values from -3.5 to 3.5
- proj_out: bfloat16 [1024, 1024], P('tensor'), may hold values from -0.1875 to 0.1875
- gain_ffn: float32 [1024], replicated, may hold values from 0.5 to 1.5
- w_gate: bfloat16 [1024, 4608], P(None, 'tensor'), may hold values from -0.1875 to 0.1875
- w_up: bfloat16 [1024, 4608], P(None, 'tensor'), may hold values from -0.1875 to 0.1875
- w_down: bfloat16 [4608, 1024], P('tensor'), may hold values from -0.125 to 0.125
- cotangent: bfloat16 [32768, 1024], P(('dp', 'tensor')), may hold values from -6 to 6
Outputs:
- output: bfloat16 [32768, 1024], P(('dp', 'tensor'))
- grad_tokens: float32 [32768, 1024], P(('dp', 'tensor'))
- grad_gain_mix: float32 [1024], replicated
- grad_proj_in: float32 [1024, 3, 1024], P(None, None, 'tensor')
- grad_conv_filter: float32 [3, 1024], P(None, 'tensor')
- grad_proj_out: float32 [1024, 1024], P('tensor')
- grad_gain_ffn: float32 [1024], replicated
- grad_w_gate: float32 [1024, 4608], P(None, 'tensor')
- grad_w_up: float32 [1024, 4608], P(None, 'tensor')
- grad_w_down: float32 [4608, 1024], P('tensor')
The draws below stay inside these ranges and needn't reach their ends.
All inputs are finite; a program needn't handle non-finite values.
Results may differ from the reference program's by a relative error of at most 0.0099.
Values may be sent and summed in bfloat16 or wider, within the bound.
No kernel may reach another device: no remote copies, remote signals or barrier semaphores. Data moves between devices by JAX's collectives and lax.ppermute only.
A program may use at most 256 MiB of HBM per device.

```python
import jax
import jax.numpy as jnp
from jax import lax

D = 1024
FF = 4608
KW = 3
LEN = 512
SEQ_DEV = 4
TOKENS = 32768


def level_of(key, dims, split, low, largest):
    factor_of, own = 1.0, jax.random.fold_in(key, 6)
    for dim, shards_of in split:
        draws = jnp.exp(jax.random.uniform(jax.random.fold_in(own, dim), (shards_of,), jnp.float32, low / len(split), largest / len(split)))
        factor_of = factor_of * jnp.repeat(draws, dims[dim] // shards_of).reshape([-1 if axis == dim else 1 for axis in range(len(dims))])
    return factor_of


def bell_draw(stream_key, dims, width, bound, split=(), kind=jnp.bfloat16):
    values = jax.random.normal(stream_key, dims, jnp.float32) * width
    if len(split) > 0:
        values = level_of(stream_key, dims, split, -0.22, 0.18) * values
    return jnp.clip(values, min=-bound, max=bound).astype(kind)


def setup_inputs(seed: int = 0) -> dict:
    key_list = jax.random.split(jax.random.key(seed), 11)
    return {
        "tokens": bell_draw(key_list[0], (TOKENS, D), 1.0, 6.0, ((0, 32),)),
        "gain_mix": jnp.clip(1.0 + 0.1 * jax.random.normal(key_list[1], (D,), jnp.float32), 0.5, 1.5),
        "proj_in": bell_draw(key_list[2], (D, 3, D), D ** -0.5, 0.1875, ((2, 2),)),
        "conv_filter": bell_draw(key_list[3], (KW, D), KW ** -0.5, 3.5, ((1, 2),), jnp.float32),
        "proj_out": bell_draw(key_list[4], (D, D), D ** -0.5, 0.1875, ((0, 2),)),
        "gain_ffn": jnp.clip(1.0 + 0.1 * jax.random.normal(key_list[5], (D,), jnp.float32), 0.5, 1.5),
        "w_gate": bell_draw(key_list[6], (D, FF), D ** -0.5, 0.1875, ((1, 2),)),
        "w_up": bell_draw(key_list[7], (D, FF), D ** -0.5, 0.1875, ((1, 2),)),
        "w_down": bell_draw(key_list[8], (FF, D), (FF // 2) ** -0.5, 0.125, ((0, 2),)),
        "cotangent": bell_draw(key_list[9], (TOKENS, D), 1.0, 6.0, ((0, 32),)),
    }


epsilon = 1e-05

@jax.custom_vjp
def low(v):
    return lax.optimization_barrier(v.astype(jnp.bfloat16)).astype(jnp.float32)

@jax.custom_vjp
def low_back(v):
    return v

def low_keep(v):
    return (low(v), None)

def low_pass(kept, grad):
    return (grad,)

def back_keep(v):
    return (v, None)

def back_low(kept, grad):
    return (low(grad),)
low.defvjp(low_keep, low_pass)
low_back.defvjp(back_keep, back_low)

def product(left, right):
    return jnp.dot(left, right, precision=lax.Precision.HIGHEST, preferred_element_type=jnp.float32)

def rms_scale(values):
    return lax.rsqrt(lax.optimization_barrier(jnp.mean(values * values, axis=-1, keepdims=True)) + epsilon)

def shift_down(values, steps):
    position = (jnp.arange(values.shape[0]) % LEN)[:, None]
    shifted = jnp.concatenate([jnp.zeros((steps, values.shape[1]), values.dtype), values[:-steps]], 0)
    return jnp.where(position >= steps, shifted, jnp.zeros_like(shifted))

def forward(tokens, gain_mix, proj_in, conv_filter, proj_out, gain_ffn, w_gate, w_up, w_down):
    model_width = tokens.shape[1]
    normed = low(tokens * rms_scale(tokens) * gain_mix)
    projected = low_back(product(normed, proj_in.reshape(model_width, 3 * model_width)))
    projected = projected.reshape(-1, 3, model_width)
    gate_b = projected[:, 0]
    gate_c = projected[:, 1]
    values = projected[:, 2]
    mixed_in = gate_b * values
    convolved = conv_filter[2] * mixed_in + conv_filter[1] * shift_down(mixed_in, 1) + conv_filter[0] * shift_down(mixed_in, 2)
    gated = low(gate_c * convolved)
    mixer = low_back(product(gated, proj_out))
    middle = tokens + mixer
    normed_mid = low(middle * rms_scale(middle) * gain_ffn)
    gate_value = low_back(product(normed_mid, w_gate))
    up_value = low_back(product(normed_mid, w_up))
    hidden = low(jax.nn.silu(gate_value) * up_value)
    return middle + low_back(product(hidden, w_down))

def reference(tokens, gain_mix, proj_in, conv_filter, proj_out, gain_ffn, w_gate, w_up, w_down, cotangent):
    group_rows = SEQ_DEV * LEN
    groups = tokens.shape[0] // group_rows
    model_width = tokens.shape[1]
    inputs = tokens.astype(jnp.float32).reshape(groups, group_rows, model_width)
    cot_groups = cotangent.astype(jnp.float32).reshape(groups, group_rows, model_width)
    weights = tuple((w.astype(jnp.float32) for w in (gain_mix, proj_in, conv_filter, proj_out, gain_ffn, w_gate, w_up, w_down)))

    def group_step(totals, group_pair):
        group_in, group_cot = group_pair
        result, pull_back = jax.vjp(forward, group_in, *weights)
        gradients = pull_back(group_cot)
        return (tuple((a + b for a, b in zip(totals, gradients[1:]))), (result, gradients[0]))
    start_totals = tuple((jnp.zeros(w.shape, jnp.float32) for w in weights))
    totals, stacked = lax.scan(group_step, start_totals, (inputs, cot_groups))
    output = stacked[0].reshape(-1, model_width).astype(jnp.bfloat16)
    grad_tokens = stacked[1].reshape(-1, model_width)
    return (output, grad_tokens, totals[0], totals[1], totals[2], totals[3], totals[4], totals[5], totals[6], totals[7])
```

```python
import functools

import jax
import jax.numpy as jnp
from jax import lax
from jax.experimental import pallas as pl
from jax.experimental.pallas import tpu as pltpu
from jax.sharding import PartitionSpec as P

LEN = 512


epsilon = 1e-05


def times_rows(left, right):
    return jnp.dot(left, right, preferred_element_type=jnp.float32)


def left_outer(left, right):
    return lax.dot_general(
        left, right, (((0,), (0,)), ((), ())), preferred_element_type=jnp.float32
    )


def right_outer(left, right):
    return lax.dot_general(
        left, right, (((1,), (1,)), ((), ())), preferred_element_type=jnp.float32
    )


def row_position(values):
    return lax.broadcasted_iota(jnp.int32, (values.shape[0], 1), 0) % LEN


def shift_down(values, steps):
    shifted = jnp.concatenate(
        [jnp.zeros((steps, values.shape[1]), values.dtype), values[:-steps]], 0
    )
    return jnp.where(row_position(values) >= steps, shifted, jnp.zeros_like(shifted))


def shift_up(values, steps):
    masked = jnp.where(row_position(values) >= steps, values, jnp.zeros_like(values))
    return jnp.concatenate([masked[steps:], jnp.zeros((steps, values.shape[1]), values.dtype)], 0)


def norm_back(grad_unit, unit, scale):
    return scale * (grad_unit - unit * jnp.mean(grad_unit * unit, axis=-1, keepdims=True))


def split_shards(
    tokens, gain_mix, proj_in, conv_filter, proj_out, gain_ffn, w_gate, w_up, w_down, cotangent
):
    model_width = tokens.shape[1]
    channels = proj_in.shape[2]
    resid_in = tokens.astype(jnp.float32)
    scale_mix = lax.rsqrt(jnp.mean(resid_in * resid_in, axis=-1, keepdims=True) + epsilon)
    unit_mix = resid_in * scale_mix
    normed = (unit_mix * gain_mix).astype(jnp.bfloat16)
    normed_all = lax.all_gather(normed, "tensor", axis=0, tiled=True)
    flat_in = proj_in.reshape(model_width, 3 * channels)
    projected = times_rows(normed_all, flat_in).reshape(-1, 3, channels)
    gate_b = projected[:, 0]
    gate_c = projected[:, 1]
    values = projected[:, 2]
    mixed_in = gate_b * values
    back_one = shift_down(mixed_in, 1)
    back_two = shift_down(mixed_in, 2)
    convolved = conv_filter[2] * mixed_in + conv_filter[1] * back_one + conv_filter[0] * back_two
    gated = (gate_c * convolved).astype(jnp.bfloat16)
    mixer = lax.psum_scatter(times_rows(gated, proj_out), "tensor", scatter_dimension=0, tiled=True)
    middle = resid_in + mixer
    scale_ffn = lax.rsqrt(jnp.mean(middle * middle, axis=-1, keepdims=True) + epsilon)
    unit_ffn = middle * scale_ffn
    normed_mid = (unit_ffn * gain_ffn).astype(jnp.bfloat16)
    grad_out = cotangent.astype(jnp.float32)
    mid_all = lax.all_gather(normed_mid, "tensor", axis=0, tiled=True)
    gate_value = times_rows(mid_all, w_gate)
    up_value = times_rows(mid_all, w_up)
    sigmoid_gate = jax.nn.sigmoid(gate_value)
    hidden = (gate_value * sigmoid_gate * up_value).astype(jnp.bfloat16)
    branch = lax.psum_scatter(times_rows(hidden, w_down), "tensor", scatter_dimension=0, tiled=True)
    cot_all = lax.all_gather(cotangent, "tensor", axis=0, tiled=True)
    grad_hidden = right_outer(cot_all, w_down)
    grad_gate = (
        grad_hidden * up_value * sigmoid_gate * (1.0 + gate_value * (1.0 - sigmoid_gate))
    ).astype(jnp.bfloat16)
    grad_upper = (grad_hidden * gate_value * sigmoid_gate).astype(jnp.bfloat16)
    grad_w_down = left_outer(hidden, cot_all)
    grad_w_gate = left_outer(mid_all, grad_gate)
    grad_w_up = left_outer(mid_all, grad_upper)
    grad_mid = lax.psum_scatter(
        right_outer(grad_gate, w_gate) + right_outer(grad_upper, w_up),
        "tensor",
        scatter_dimension=0,
        tiled=True,
    )
    output = (middle + branch).astype(jnp.bfloat16)
    grad_gain_ffn = jnp.sum(grad_mid * unit_ffn, axis=0)
    grad_middle = grad_out + norm_back(grad_mid * gain_ffn, unit_ffn, scale_ffn)
    mixer_cot = grad_middle.astype(jnp.bfloat16)
    cot_mix_all = lax.all_gather(mixer_cot, "tensor", axis=0, tiled=True)
    grad_proj_out = left_outer(gated, cot_mix_all)
    grad_gated = right_outer(cot_mix_all, proj_out)
    grad_cgate = grad_gated * convolved
    grad_conv = grad_gated * gate_c
    grad_conv_filter = jnp.stack(
        [
            jnp.sum(grad_conv * back_two, axis=0),
            jnp.sum(grad_conv * back_one, axis=0),
            jnp.sum(grad_conv * mixed_in, axis=0),
        ],
        0,
    )
    grad_mixed = (
        conv_filter[2] * grad_conv
        + conv_filter[1] * shift_up(grad_conv, 1)
        + conv_filter[0] * shift_up(grad_conv, 2)
    )
    grad_proj = (
        jnp.stack([grad_mixed * values, grad_cgate, grad_mixed * gate_b], 1)
        .astype(jnp.bfloat16)
        .reshape(-1, 3 * channels)
    )
    grad_proj_in = left_outer(normed_all, grad_proj).reshape(model_width, 3, channels)
    grad_normed = lax.psum_scatter(
        right_outer(grad_proj, flat_in), "tensor", scatter_dimension=0, tiled=True
    )
    grad_gain_mix = jnp.sum(grad_normed * unit_mix, axis=0)
    grad_tokens = grad_middle + norm_back(grad_normed * gain_mix, unit_mix, scale_mix)
    grad_gain_mix, grad_gain_ffn = lax.psum((grad_gain_mix, grad_gain_ffn), ("dp", "tensor"))
    grad_proj_in, grad_conv_filter, grad_proj_out, grad_w_gate, grad_w_up, grad_w_down = lax.psum(
        (grad_proj_in, grad_conv_filter, grad_proj_out, grad_w_gate, grad_w_up, grad_w_down), "dp"
    )
    return (
        output,
        grad_tokens,
        grad_gain_mix,
        grad_proj_in,
        grad_conv_filter,
        grad_proj_out,
        grad_gain_ffn,
        grad_w_gate,
        grad_w_up,
        grad_w_down,
    )


WIDE = 256
ROW_TILE = 512
GROUPS = (4, 5)
MIB = 1024 * 1024


def fits(sizes, args):
    dp, tensor = sizes
    tokens, proj_in, w_gate = args[0], args[2], args[6]
    return (
        tensor == 2
        and dp & (dp - 1) == 0
        and 2 <= dp <= 16
        and tokens.shape[0] % LEN == 0
        and tokens.shape[1] == 1024
        and proj_in.shape[2] % 128 == 0
        and w_gate.shape[1] == WIDE * sum(GROUPS)
    )


def ffn_body(first, *refs):
    if first:
        h, ht, e, et, wg, wu, wd, branch, grad_h, keep, send, zs, gg, gu = refs
    else:
        h, ht, e, et, wg, wu, wd, branch_in, grad_in, branch, grad_h, keep, send, zs, gg, gu = refs
    rows, half, wide = h.shape[0], keep.shape[0], wg.shape[1]

    @pl.when(pl.program_id(0) == 0)
    def _():
        if first:
            branch[...] = jnp.zeros_like(branch)
            grad_h[...] = jnp.zeros_like(grad_h)
        else:
            branch[...] = branch_in[...]
            grad_h[...] = grad_in[...]

    for start in range(0, rows, ROW_TILE):
        r = pl.ds(start, ROW_TILE)
        gate = times_rows(h[r, :], wg[...])
        up = times_rows(h[r, :], wu[...])
        grad_hidden = right_outer(e[r, :], wd[...])
        s = jax.nn.sigmoid(gate)
        gs = gate * s
        hidden = (gs * up).astype(jnp.bfloat16)
        grad_up = (grad_hidden * gs).astype(jnp.bfloat16)
        grad_gate = (grad_hidden * up * (s + gs * (1.0 - s))).astype(jnp.bfloat16)
        zs[r, :] = hidden
        gg[r, :] = grad_gate
        gu[r, :] = grad_up
        branch[r, :] += times_rows(hidden, wd[...])
        grad_h[r, :] += right_outer(grad_gate, wg[...]) + right_outer(grad_up, wu[...])
    for out, base in ((keep, 0), (send, half)):
        a = ht[pl.ds(base, half), :]
        out[:, 0:wide] = times_rows(a, gg[...]).astype(jnp.bfloat16)
        out[:, wide : 2 * wide] = times_rows(a, gu[...]).astype(jnp.bfloat16)
        out[:, 2 * wide : 3 * wide] = times_rows(et[pl.ds(base, half), :], zs[...]).astype(jnp.bfloat16)


def ffn_part(h, ht, e, et, wg, wu, wd, sums, gate_at, down_at, count):
    rows, width = h.shape
    first = sums is None

    def whole(shape):
        return pl.BlockSpec(shape, lambda j: (0, 0), pipeline_mode=pl.Buffered(1))

    in_specs = [
        whole((rows, width)),
        whole((width, rows)),
        whole((rows, width)),
        whole((width, rows)),
        pl.BlockSpec((width, WIDE), lambda j: (0, gate_at + j)),
        pl.BlockSpec((width, WIDE), lambda j: (0, gate_at + j)),
        pl.BlockSpec((WIDE, width), lambda j: (down_at + j, 0)),
    ]
    args = [h, ht, e, et, wg, wu, wd]
    if not first:
        in_specs += [whole((rows, width))] * 2
        args += list(sums)
    branch, grad_h, keep, send = pl.pallas_call(
        functools.partial(ffn_body, first),
        grid=(count,),
        in_specs=in_specs,
        out_specs=[pl.BlockSpec((rows, width), lambda j: (0, 0))] * 2
        + [pl.BlockSpec((width // 2, 3 * WIDE), lambda j: (0, j))] * 2,
        out_shape=[jax.ShapeDtypeStruct((rows, width), jnp.float32)] * 2
        + [jax.ShapeDtypeStruct((width // 2, 3 * WIDE * count), jnp.bfloat16)] * 2,
        scratch_shapes=[pltpu.VMEM((rows, WIDE), jnp.bfloat16)] * 3,
        input_output_aliases={} if first else {7: 0, 8: 1},
        compiler_params=pltpu.CompilerParams(vmem_limit_bytes=56 * MIB),
        cost_estimate=pl.CostEstimate(
            flops=20 * rows * width * WIDE * count,
            bytes_accessed=12 * width * WIDE * count + 16 * rows * width,
            transcendentals=rows * WIDE * count,
        ),
    )(*args)
    return (branch, grad_h), (keep, send)


def ffn_final_body(grads, *refs):
    gate, up, down = refs[-3:]
    gate[...] = grads[:, 0:WIDE].astype(jnp.float32)
    up[...] = grads[:, WIDE : 2 * WIDE].astype(jnp.float32)
    down[...] = grads[:, 2 * WIDE : 3 * WIDE].astype(jnp.float32).T


def ffn_final(grads, totals, at, columns):
    width = grads.shape[0]
    count = grads.shape[1] // (3 * WIDE)
    old = [] if totals is None else list(totals)
    return pl.pallas_call(
        ffn_final_body,
        grid=(count,),
        in_specs=[pl.BlockSpec((width, 3 * WIDE), lambda j: (0, j))]
        + [pl.BlockSpec(memory_space=pl.ANY)] * len(old),
        out_specs=[
            pl.BlockSpec((width, WIDE), lambda j: (0, at + j)),
            pl.BlockSpec((width, WIDE), lambda j: (0, at + j)),
            pl.BlockSpec((WIDE, width), lambda j: (at + j, 0)),
        ],
        out_shape=[
            jax.ShapeDtypeStruct((width, columns), jnp.float32),
            jax.ShapeDtypeStruct((width, columns), jnp.float32),
            jax.ShapeDtypeStruct((columns, width), jnp.float32),
        ],
        input_output_aliases={1 + i: i for i in range(len(old))},
        compiler_params=pltpu.CompilerParams(vmem_limit_bytes=40 * MIB),
        cost_estimate=pl.CostEstimate(
            flops=0, bytes_accessed=18 * width * WIDE * count, transcendentals=0
        ),
    )(grads, *old)


def swap(values, dp, bit):
    return lax.ppermute(values, "dp", [(i, i ^ (1 << bit)) for i in range(dp)])


def cross(values):
    return lax.ppermute(values, "tensor", [(0, 1), (1, 0)])


def add(*terms):
    total = terms[0].astype(jnp.float32)
    for term in terms[1:]:
        total = total + term.astype(jnp.float32)
    return total.astype(terms[0].dtype)


def halve(terms, dp, bits):
    for bit in bits:
        half = terms[0].shape[0] // 2
        got = swap(add(*[t[half:] for t in terms]), dp, bit)
        terms = [add(*[t[:half] for t in terms]), got]
    return add(*terms)


def block_order(me, dp, width, bits):
    rows = lax.broadcasted_iota(jnp.int32, (width, width), 0)
    columns = lax.broadcasted_iota(jnp.int32, (width, width), 1)
    size = width // dp
    block = rows // size
    owner = jnp.zeros_like(block)
    for place, bit in enumerate(reversed(bits)):
        owner = owner | (((block >> place) & 1) << bit)
    return (columns == (owner ^ me) * size + rows % size).astype(jnp.bfloat16)


def ordered(order, values):
    return right_outer(order, values).astype(jnp.bfloat16)


def mixer_forward(normed, flat_in, taps):
    channels = taps.shape[1]
    projected = times_rows(normed, flat_in)
    gate_b = projected[:, :channels]
    gate_c = projected[:, channels : 2 * channels]
    values = projected[:, 2 * channels :]
    mixed_in = gate_b * values
    back_one = shift_down(mixed_in, 1)
    back_two = shift_down(mixed_in, 2)
    convolved = taps[2] * mixed_in + taps[1] * back_one + taps[0] * back_two
    gated = (gate_c * convolved).astype(jnp.bfloat16)
    return gate_b, gate_c, values, mixed_in, back_one, back_two, convolved, gated


def mixer_backward(grad_gated, kept, taps):
    gate_b, gate_c, values, mixed_in, back_one, back_two, convolved, _ = kept
    grad_cgate = grad_gated * convolved
    grad_conv = grad_gated * gate_c
    grad_taps = jnp.stack(
        [
            jnp.sum(grad_conv * back_two, axis=0),
            jnp.sum(grad_conv * back_one, axis=0),
            jnp.sum(grad_conv * mixed_in, axis=0),
        ],
        0,
    )
    grad_mixed = taps[2] * grad_conv + taps[1] * shift_up(grad_conv, 1) + taps[0] * shift_up(grad_conv, 2)
    grad_proj = jnp.concatenate(
        [grad_mixed * values, grad_cgate, grad_mixed * gate_b], 1
    ).astype(jnp.bfloat16)
    return grad_taps, grad_proj


def paired_shards(
    dp, tokens, gain_mix, proj_in, taps, proj_out, gain_ffn, w_gate, w_up, w_down, cotangent
):
    me = lax.axis_index("dp")
    core = me & 1
    width = tokens.shape[1]
    channels = proj_in.shape[2]
    hidden = w_gate.shape[1]
    bits = tuple(range(dp.bit_length() - 1))
    flat_in = proj_in.reshape(width, 3 * channels)

    def far_blocks(values):
        size = values.shape[0] // dp
        return cross(lax.dynamic_slice_in_dim(values, me * size, size, 0))

    def gathered(blocks):
        return lax.all_gather(blocks, "dp", axis=0, tiled=True)

    in_blocks, out_blocks, down_blocks = far_blocks(flat_in), far_blocks(proj_out), far_blocks(w_down)
    taps_far = cross(taps)
    flat_in_far = gathered(in_blocks)
    proj_out_far = gathered(out_blocks)
    w_down_far = gathered(down_blocks)

    def far_columns(values, at, count, after):
        part = lax.dynamic_slice(values, (core * (width // 2), at), (width // 2, count))
        part, _ = lax.optimization_barrier((part, after))
        mine = cross(part)
        other = swap(mine, dp, 0)
        return jnp.concatenate([jnp.where(core == 0, mine, other), jnp.where(core == 0, other, mine)], 0)

    far, at, after = [], 0, (in_blocks, out_blocks, down_blocks)
    for count in GROUPS:
        gate_far = far_columns(w_gate, at * WIDE, count * WIDE, after)
        up_far = far_columns(w_up, at * WIDE, count * WIDE, after)
        far.append((gate_far, up_far))
        at += count

    order = block_order(me, dp, width, bits)
    cot_t = ordered(order, cotangent)

    resid_in = tokens.astype(jnp.float32)
    scale_mix = lax.rsqrt(jnp.mean(resid_in * resid_in, axis=-1, keepdims=True) + epsilon)
    unit_mix = resid_in * scale_mix
    normed = (unit_mix * gain_mix).astype(jnp.bfloat16)
    normed_t = ordered(order, normed)
    kept = mixer_forward(normed, flat_in, taps)
    kept_far = mixer_forward(normed, flat_in_far, taps_far)
    mixer = times_rows(kept[-1], proj_out) + times_rows(kept_far[-1], proj_out_far)
    middle = resid_in + mixer
    scale_ffn = lax.rsqrt(jnp.mean(middle * middle, axis=-1, keepdims=True) + epsilon)
    unit_ffn = middle * scale_ffn
    normed_mid = (unit_ffn * gain_ffn).astype(jnp.bfloat16)
    normed_mid_t = ordered(order, normed_mid)

    sums, near_grads, far_grads, at = None, [], [], 0
    for count in GROUPS:
        sums, grads = ffn_part(
            normed_mid, normed_mid_t, cotangent, cot_t, w_gate, w_up, w_down, sums, at, at, count
        )
        near_grads.append(grads)
        at += count
    at = 0
    for count, (gate_far, up_far) in zip(GROUPS, far):
        sums, grads = ffn_part(
            normed_mid, normed_mid_t, cotangent, cot_t, gate_far, up_far, w_down_far, sums, 0, at, count
        )
        far_grads.append(grads)
        at += count

    def reduced(near, far, far_first):
        near = [near[0], swap(near[1], dp, bits[0])]
        far = [far[0], swap(far[1], dp, bits[0])]
        if far_first:
            return gathered(halve(near + [cross(add(*far))], dp, bits[1:]))
        return gathered(add(halve(near, dp, bits[1:]), cross(halve(far, dp, bits[1:]))))

    totals, at = None, 0
    for index, count in enumerate(GROUPS):
        grads = reduced(near_grads[index], far_grads[index], FAR_FIRST[index])
        totals = ffn_final(grads, totals, at, hidden)
        at += count
    grad_w_gate, grad_w_up, grad_w_down = totals

    branch, grad_mid = sums
    output = (middle + branch).astype(jnp.bfloat16)
    grad_gain_ffn = jnp.sum(grad_mid * unit_ffn, axis=0)
    grad_middle = cotangent.astype(jnp.float32) + norm_back(grad_mid * gain_ffn, unit_ffn, scale_ffn)
    mixer_cot = grad_middle.astype(jnp.bfloat16)
    mixer_cot_t = ordered(order, mixer_cot)
    grad_taps, grad_proj = mixer_backward(right_outer(mixer_cot, proj_out), kept, taps)
    grad_taps_far, grad_proj_far = mixer_backward(right_outer(mixer_cot, proj_out_far), kept_far, taps_far)

    def mixer_grads(grad_proj, gated):
        def rows(part):
            return jnp.concatenate(
                [times_rows(normed_t[part], grad_proj), times_rows(mixer_cot_t[part], gated)], 1
            ).astype(jnp.bfloat16)

        return rows(slice(0, width // 2)), rows(slice(width // 2, width))

    grads = reduced(
        mixer_grads(grad_proj, kept[-1]), mixer_grads(grad_proj_far, kept_far[-1]), FAR_FIRST[-1]
    )
    grad_proj_in = grads[:, : 3 * channels].astype(jnp.float32).reshape(width, 3, channels)
    grad_proj_out = grads[:, 3 * channels :].astype(jnp.float32).T

    grad_normed = right_outer(grad_proj, flat_in) + right_outer(grad_proj_far, flat_in_far)
    grad_gain_mix = jnp.sum(grad_normed * unit_mix, axis=0)
    grad_tokens = grad_middle + norm_back(grad_normed * gain_mix, unit_mix, scale_mix)

    gains = jnp.concatenate([grad_gain_mix[None], grad_gain_ffn[None]], 0)
    small = jnp.concatenate([gains[:, :channels], gains[:, channels:], grad_taps], 0)
    small_far = jnp.concatenate([gains[:, :channels], gains[:, channels:], grad_taps_far], 0)
    small = small + cross(small_far)
    for bit in bits:
        small = small + swap(small, dp, bit)
    gains = jnp.concatenate([small[0:2], small[2:4]], 1)
    return (
        output,
        grad_tokens,
        gains[0],
        grad_proj_in,
        small[4:7],
        grad_proj_out,
        gains[1],
        grad_w_gate,
        grad_w_up,
        grad_w_down,
    )


FAR_FIRST = (True, False, True)


def solution(mesh):
    placed = (
        P(("dp", "tensor"), None),
        P(),
        P(None, None, "tensor"),
        P(None, "tensor"),
        P("tensor", None),
        P(),
        P(None, "tensor"),
        P(None, "tensor"),
        P("tensor", None),
        P(("dp", "tensor"), None),
    )
    sizes = (mesh.shape["dp"], mesh.shape["tensor"])

    def block(*args):
        if fits(sizes, args):
            return paired_shards(sizes[0], *args)
        return split_shards(*args)

    return jax.shard_map(
        block,
        mesh=mesh,
        in_specs=placed,
        out_specs=(
            P(("dp", "tensor"), None),
            P(("dp", "tensor"), None),
            P(),
            P(None, None, "tensor"),
            P(None, "tensor"),
            P("tensor", None),
            P(),
            P(None, "tensor"),
            P(None, "tensor"),
            P("tensor", None),
        ),
        check_vma=False,
    )
```

```python
import functools

import jax
import jax.numpy as jnp
from jax import lax
from jax.experimental import pallas as pl
from jax.experimental.pallas import tpu as pltpu
from jax.sharding import PartitionSpec as P

LEN = 512


epsilon = 1e-05


def times_rows(left, right):
    return jnp.dot(left, right, preferred_element_type=jnp.float32)


def left_outer(left, right):
    return lax.dot_general(
        left, right, (((0,), (0,)), ((), ())), preferred_element_type=jnp.float32
    )


def right_outer(left, right):
    return lax.dot_general(
        left, right, (((1,), (1,)), ((), ())), preferred_element_type=jnp.float32
    )


def row_position(values):
    return lax.broadcasted_iota(jnp.int32, (values.shape[0], 1), 0) % LEN


def shift_down(values, steps):
    shifted = jnp.concatenate(
        [jnp.zeros((steps, values.shape[1]), values.dtype), values[:-steps]], 0
    )
    return jnp.where(row_position(values) >= steps, shifted, jnp.zeros_like(shifted))


def shift_up(values, steps):
    masked = jnp.where(row_position(values) >= steps, values, jnp.zeros_like(values))
    return jnp.concatenate([masked[steps:], jnp.zeros((steps, values.shape[1]), values.dtype)], 0)


def norm_back(grad_unit, unit, scale):
    return scale * (grad_unit - unit * jnp.mean(grad_unit * unit, axis=-1, keepdims=True))


def split_shards(
    tokens, gain_mix, proj_in, conv_filter, proj_out, gain_ffn, w_gate, w_up, w_down, cotangent
):
    model_width = tokens.shape[1]
    channels = proj_in.shape[2]
    resid_in = tokens.astype(jnp.float32)
    scale_mix = lax.rsqrt(jnp.mean(resid_in * resid_in, axis=-1, keepdims=True) + epsilon)
    unit_mix = resid_in * scale_mix
    normed = (unit_mix * gain_mix).astype(jnp.bfloat16)
    normed_all = lax.all_gather(normed, "tensor", axis=0, tiled=True)
    flat_in = proj_in.reshape(model_width, 3 * channels)
    projected = times_rows(normed_all, flat_in).reshape(-1, 3, channels)
    gate_b = projected[:, 0]
    gate_c = projected[:, 1]
    values = projected[:, 2]
    mixed_in = gate_b * values
    back_one = shift_down(mixed_in, 1)
    back_two = shift_down(mixed_in, 2)
    convolved = conv_filter[2] * mixed_in + conv_filter[1] * back_one + conv_filter[0] * back_two
    gated = (gate_c * convolved).astype(jnp.bfloat16)
    mixer = lax.psum_scatter(times_rows(gated, proj_out), "tensor", scatter_dimension=0, tiled=True)
    middle = resid_in + mixer
    scale_ffn = lax.rsqrt(jnp.mean(middle * middle, axis=-1, keepdims=True) + epsilon)
    unit_ffn = middle * scale_ffn
    normed_mid = (unit_ffn * gain_ffn).astype(jnp.bfloat16)
    grad_out = cotangent.astype(jnp.float32)
    mid_all = lax.all_gather(normed_mid, "tensor", axis=0, tiled=True)
    gate_value = times_rows(mid_all, w_gate)
    up_value = times_rows(mid_all, w_up)
    sigmoid_gate = jax.nn.sigmoid(gate_value)
    hidden = (gate_value * sigmoid_gate * up_value).astype(jnp.bfloat16)
    branch = lax.psum_scatter(times_rows(hidden, w_down), "tensor", scatter_dimension=0, tiled=True)
    cot_all = lax.all_gather(cotangent, "tensor", axis=0, tiled=True)
    grad_hidden = right_outer(cot_all, w_down)
    grad_gate = (
        grad_hidden * up_value * sigmoid_gate * (1.0 + gate_value * (1.0 - sigmoid_gate))
    ).astype(jnp.bfloat16)
    grad_upper = (grad_hidden * gate_value * sigmoid_gate).astype(jnp.bfloat16)
    grad_w_down = left_outer(hidden, cot_all)
    grad_w_gate = left_outer(mid_all, grad_gate)
    grad_w_up = left_outer(mid_all, grad_upper)
    grad_mid = lax.psum_scatter(
        right_outer(grad_gate, w_gate) + right_outer(grad_upper, w_up),
        "tensor",
        scatter_dimension=0,
        tiled=True,
    )
    output = (middle + branch).astype(jnp.bfloat16)
    grad_gain_ffn = jnp.sum(grad_mid * unit_ffn, axis=0)
    grad_middle = grad_out + norm_back(grad_mid * gain_ffn, unit_ffn, scale_ffn)
    mixer_cot = grad_middle.astype(jnp.bfloat16)
    cot_mix_all = lax.all_gather(mixer_cot, "tensor", axis=0, tiled=True)
    grad_proj_out = left_outer(gated, cot_mix_all)
    grad_gated = right_outer(cot_mix_all, proj_out)
    grad_cgate = grad_gated * convolved
    grad_conv = grad_gated * gate_c
    grad_conv_filter = jnp.stack(
        [
            jnp.sum(grad_conv * back_two, axis=0),
            jnp.sum(grad_conv * back_one, axis=0),
            jnp.sum(grad_conv * mixed_in, axis=0),
        ],
        0,
    )
    grad_mixed = (
        conv_filter[2] * grad_conv
        + conv_filter[1] * shift_up(grad_conv, 1)
        + conv_filter[0] * shift_up(grad_conv, 2)
    )
    grad_proj = (
        jnp.stack([grad_mixed * values, grad_cgate, grad_mixed * gate_b], 1)
        .astype(jnp.bfloat16)
        .reshape(-1, 3 * channels)
    )
    grad_proj_in = left_outer(normed_all, grad_proj).reshape(model_width, 3, channels)
    grad_normed = lax.psum_scatter(
        right_outer(grad_proj, flat_in), "tensor", scatter_dimension=0, tiled=True
    )
    grad_gain_mix = jnp.sum(grad_normed * unit_mix, axis=0)
    grad_tokens = grad_middle + norm_back(grad_normed * gain_mix, unit_mix, scale_mix)
    grad_gain_mix, grad_gain_ffn = lax.psum((grad_gain_mix, grad_gain_ffn), ("dp", "tensor"))
    grad_proj_in, grad_conv_filter, grad_proj_out, grad_w_gate, grad_w_up, grad_w_down = lax.psum(
        (grad_proj_in, grad_conv_filter, grad_proj_out, grad_w_gate, grad_w_up, grad_w_down), "dp"
    )
    return (
        output,
        grad_tokens,
        grad_gain_mix,
        grad_proj_in,
        grad_conv_filter,
        grad_proj_out,
        grad_gain_ffn,
        grad_w_gate,
        grad_w_up,
        grad_w_down,
    )


WIDE = 256
ROW_TILE = 512
GROUPS = (3, 3, 3)
MIB = 1024 * 1024


def fits(sizes, args):
    dp, tensor = sizes
    tokens, proj_in, w_gate = args[0], args[2], args[6]
    return (
        tensor == 2
        and dp & (dp - 1) == 0
        and 4 <= dp <= 16
        and tokens.shape[0] % LEN == 0
        and tokens.shape[1] == 1024
        and proj_in.shape[2] % 128 == 0
        and w_gate.shape[1] == WIDE * sum(GROUPS)
    )


def ffn_body(h, ht, e, et, wg, wu, wd, branch, grad_h, keep, send, zs, gg, gu, branch_sum, grad_sum):
    rows, half, wide = h.shape[0], keep.shape[0], wg.shape[1]
    step = pl.program_id(0)

    @pl.when(step == 0)
    def _():
        branch_sum[...] = jnp.zeros_like(branch_sum)
        grad_sum[...] = jnp.zeros_like(grad_sum)

    for start in range(0, rows, ROW_TILE):
        r = pl.ds(start, ROW_TILE)
        gate = times_rows(h[r, :], wg[...])
        up = times_rows(h[r, :], wu[...])
        grad_hidden = right_outer(e[r, :], wd[...])
        s = jax.nn.sigmoid(gate)
        gs = gate * s
        hidden = (gs * up).astype(jnp.bfloat16)
        grad_up = (grad_hidden * gs).astype(jnp.bfloat16)
        grad_gate = (grad_hidden * up * (s + gs * (1.0 - s))).astype(jnp.bfloat16)
        zs[r, :] = hidden
        gg[r, :] = grad_gate
        gu[r, :] = grad_up
        branch_sum[r, :] += times_rows(hidden, wd[...])
        grad_sum[r, :] += right_outer(grad_gate, wg[...]) + right_outer(grad_up, wu[...])
    for out, base in ((keep, 0), (send, half)):
        a = ht[pl.ds(base, half), :]
        out[:, 0:wide] = times_rows(a, gg[...]).astype(jnp.bfloat16)
        out[:, wide : 2 * wide] = times_rows(a, gu[...]).astype(jnp.bfloat16)
        out[:, 2 * wide : 3 * wide] = times_rows(et[pl.ds(base, half), :], zs[...]).astype(jnp.bfloat16)

    @pl.when(step == pl.num_programs(0) - 1)
    def _():
        branch[...] = branch_sum[...].astype(jnp.bfloat16)
        grad_h[...] = grad_sum[...].astype(jnp.bfloat16)


def ffn_part(h, ht, e, et, wg, wu, wd, gate_at, up_at, down_at, count):
    rows, width = h.shape

    def whole(shape):
        return pl.BlockSpec(shape, lambda j: (0, 0), pipeline_mode=pl.Buffered(1))

    branch, grad_h, keep, send = pl.pallas_call(
        ffn_body,
        grid=(count,),
        in_specs=[
            whole((rows, width)),
            whole((width, rows)),
            whole((rows, width)),
            whole((width, rows)),
            pl.BlockSpec((width, WIDE), lambda j: (0, gate_at + j)),
            pl.BlockSpec((width, WIDE), lambda j: (0, up_at + j)),
            pl.BlockSpec((WIDE, width), lambda j: (down_at + j, 0)),
        ],
        out_specs=[pl.BlockSpec((rows, width), lambda j: (0, 0))] * 2
        + [pl.BlockSpec((width // 2, 3 * WIDE), lambda j: (0, j))] * 2,
        out_shape=[jax.ShapeDtypeStruct((rows, width), jnp.bfloat16)] * 2
        + [jax.ShapeDtypeStruct((width // 2, 3 * WIDE * count), jnp.bfloat16)] * 2,
        scratch_shapes=[pltpu.VMEM((rows, WIDE), jnp.bfloat16)] * 3
        + [pltpu.VMEM((rows, width), jnp.float32)] * 2,
        compiler_params=pltpu.CompilerParams(vmem_limit_bytes=56 * MIB),
        cost_estimate=pl.CostEstimate(
            flops=8 * rows * width * WIDE * count, bytes_accessed=MIB, transcendentals=0
        ),
    )(h, ht, e, et, wg, wu, wd)
    return (branch, grad_h), (keep, send)


def ffn_final_body(restored, *refs):
    gate, up, down = refs[-3:]
    cuts = [slice(k * WIDE, (k + 1) * WIDE) for k in range(3)]
    if restored:
        grads = refs[0]
        gate[...] = grads[:, cuts[0]].astype(jnp.float32)
        up[...] = grads[:, cuts[1]].astype(jnp.float32)
        down[...] = grads[:, cuts[2]].astype(jnp.float32).T
        return
    own, other, restore, order = refs[:4]
    half = own.shape[0]
    gate[...] = times_rows(restore[:, :half], own[:, cuts[0]]) + times_rows(restore[:, half:], other[:, cuts[0]])
    up[...] = times_rows(restore[:, :half], own[:, cuts[1]]) + times_rows(restore[:, half:], other[:, cuts[1]])
    down[...] = left_outer(own[:, cuts[2]], order[:half, :]) + left_outer(other[:, cuts[2]], order[half:, :])


def ffn_final(grads, totals, at, columns, orders):
    restored = len(grads) == 1
    width = orders[0].shape[0]
    count = grads[0].shape[1] // (3 * WIDE)
    old = [] if totals is None else list(totals)
    new = list(grads) if restored else list(grads) + list(orders)
    return pl.pallas_call(
        functools.partial(ffn_final_body, restored),
        grid=(count,),
        in_specs=[pl.BlockSpec((g.shape[0], 3 * WIDE), lambda j: (0, j)) for g in grads]
        + [pl.BlockSpec(g.shape, lambda j: (0, 0)) for g in new[len(grads) :]]
        + [pl.BlockSpec(memory_space=pl.ANY)] * len(old),
        out_specs=[
            pl.BlockSpec((width, WIDE), lambda j: (0, at + j)),
            pl.BlockSpec((width, WIDE), lambda j: (0, at + j)),
            pl.BlockSpec((WIDE, width), lambda j: (at + j, 0)),
        ],
        out_shape=[
            jax.ShapeDtypeStruct((width, columns), jnp.float32),
            jax.ShapeDtypeStruct((width, columns), jnp.float32),
            jax.ShapeDtypeStruct((columns, width), jnp.float32),
        ],
        input_output_aliases={len(new) + i: i for i in range(len(old))},
        compiler_params=pltpu.CompilerParams(vmem_limit_bytes=40 * MIB),
        cost_estimate=pl.CostEstimate(flops=MIB, bytes_accessed=MIB, transcendentals=0),
    )(*new, *old)


def swap(values, dp, bit):
    return lax.ppermute(values, "dp", [(i, i ^ (1 << bit)) for i in range(dp)])


def cross(values):
    return jax.tree.map(lambda v: lax.ppermute(v, "tensor", [(0, 1), (1, 0)]), values)


def add(*terms):
    total = terms[0].astype(jnp.float32)
    for term in terms[1:]:
        total = total + term.astype(jnp.float32)
    return total.astype(terms[0].dtype)


def after(values, *others):
    return lax.optimization_barrier((values, others))[0]


class Chain:
    def __init__(self, dp, terms, bit=0):
        self.dp, self.bit, self.terms = dp, bit, terms

    def halve(self, *others):
        half = self.terms[0].shape[0] // 2
        total = after(add(*[t[half:] for t in self.terms]), *others)
        self.bit += 1
        self.terms = [add(*[t[:half] for t in self.terms]), swap(total, self.dp, self.bit)]
        return total

    def total(self):
        return add(*self.terms)

    def settle(self, *others):
        total = after(self.total(), *others)
        self.terms = [total]
        return total

    def take(self, other, *others):
        total = after(other.total(), *others)
        self.terms = self.terms + [cross(total)]
        return total

    def take_cut(self, other, cut, *others):
        total = after(add(*[t[:, cut] for t in other.terms]), *others)
        part = Chain(self.dp, [t[:, cut] for t in self.terms] + [cross(total)], self.bit)
        return part, total

    def gather(self, *others):
        total = after(self.total(), *others)
        self.result = (lax.all_gather(total, "dp", axis=0, tiled=True),)
        return total

    def collect(self, *others):
        total = after(jnp.concatenate(self.terms, 0) if self.bit < 0 else self.total(), *others)
        self.bit = ~self.bit if self.bit >= 0 else self.bit
        self.terms = [total, swap(total, self.dp, ~self.bit)]
        self.bit += 1
        self.result = tuple(self.terms)
        return total


def mixer_final_body(own1, other1, own2, other2, restore, order, grad_in, grad_out):
    channels = grad_in.shape[2]
    half = own1.shape[0]
    low, high = restore[:, :half], restore[:, half:]
    for k, (own, other, at) in enumerate(((own1, other1, 0), (own1, other1, 1), (own2, other2, 0))):
        cut = slice(at * channels, (at + 1) * channels)
        grad_in[k] = times_rows(low, own[:, cut]) + times_rows(high, other[:, cut])
    cut = slice(channels, 2 * channels)
    grad_out[...] = left_outer(own2[:, cut], order[:half, :]) + left_outer(other2[:, cut], order[half:, :])


def mixer_final(first, second, orders):
    half, pair = first[0].shape
    width, channels, rows = 2 * half, pair // 2, 256
    return pl.pallas_call(
        mixer_final_body,
        grid=(width // rows,),
        in_specs=[pl.BlockSpec((half, pair), lambda j: (0, 0))] * 4
        + [pl.BlockSpec((rows, width), lambda j: (j, 0)), pl.BlockSpec((width, rows), lambda j: (0, j))],
        out_specs=[
            pl.BlockSpec((3, rows, channels), lambda j: (0, j, 0)),
            pl.BlockSpec((channels, rows), lambda j: (0, j)),
        ],
        out_shape=[
            jax.ShapeDtypeStruct((3, width, channels), jnp.float32),
            jax.ShapeDtypeStruct((channels, width), jnp.float32),
        ],
        compiler_params=pltpu.CompilerParams(vmem_limit_bytes=40 * MIB),
        cost_estimate=pl.CostEstimate(flops=MIB, bytes_accessed=MIB, transcendentals=0),
    )(*first, *second, *orders)


def block_order(me, dp, width, bits):
    rows = lax.broadcasted_iota(jnp.int32, (width, width), 0)
    columns = lax.broadcasted_iota(jnp.int32, (width, width), 1)
    size = width // dp
    block = rows // size
    owner = jnp.zeros_like(block)
    for place, bit in enumerate(reversed(bits)):
        owner = owner | (((block >> place) & 1) << bit)
    return (columns == (owner ^ me) * size + rows % size).astype(jnp.bfloat16)


def ordered(order, values):
    return right_outer(order, values).astype(jnp.bfloat16)


def mixer_forward(normed, flat_in, taps):
    channels = taps.shape[1]
    projected = times_rows(normed, flat_in)
    gate_b = projected[:, :channels]
    gate_c = projected[:, channels : 2 * channels]
    values = projected[:, 2 * channels :]
    mixed_in = gate_b * values
    back_one = shift_down(mixed_in, 1)
    back_two = shift_down(mixed_in, 2)
    convolved = taps[2] * mixed_in + taps[1] * back_one + taps[0] * back_two
    gated = (gate_c * convolved).astype(jnp.bfloat16)
    return gate_b, gate_c, values, mixed_in, back_one, back_two, convolved, gated


def mixer_backward(grad_gated, kept, taps):
    gate_b, gate_c, values, mixed_in, back_one, back_two, convolved, _ = kept
    grad_cgate = grad_gated * convolved
    grad_conv = grad_gated * gate_c
    grad_taps = jnp.stack(
        [
            jnp.sum(grad_conv * back_two, axis=0),
            jnp.sum(grad_conv * back_one, axis=0),
            jnp.sum(grad_conv * mixed_in, axis=0),
        ],
        0,
    )
    grad_mixed = taps[2] * grad_conv + taps[1] * shift_up(grad_conv, 1) + taps[0] * shift_up(grad_conv, 2)
    grad_proj = jnp.concatenate(
        [grad_mixed * values, grad_cgate, grad_mixed * gate_b], 1
    ).astype(jnp.bfloat16)
    return grad_taps, grad_proj


def paired_shards(
    dp, tokens, gain_mix, proj_in, taps, proj_out, gain_ffn, w_gate, w_up, w_down, cotangent
):
    me = lax.axis_index("dp")
    core = me & 1
    width = tokens.shape[1]
    channels = proj_in.shape[2]
    hidden = w_gate.shape[1]
    bits = tuple(range(dp.bit_length() - 1))

    def gathered(blocks):
        return lax.all_gather(blocks, "dp", axis=0, tiled=True)

    half = width // 2
    def my_rows(values):
        size = values.shape[0] // dp
        return lax.dynamic_slice_in_dim(values, me * size, size, 0)

    in_blocks = cross(my_rows(proj_in).reshape(width // dp, 3 * channels))
    out_half = cross(lax.dynamic_slice_in_dim(proj_out, core * (channels // 2), channels // 2, 0))
    taps_far = cross(taps)
    flat_in_far = gathered(in_blocks)
    late = GROUPS[0] * WIDE

    def far_join(mine, axis):
        other = swap(mine, dp, 0)
        return jnp.concatenate([jnp.where(core == 0, mine, other), jnp.where(core == 0, other, mine)], axis)

    def gate_part(at, count):
        return jnp.concatenate(
            [lax.dynamic_slice(w, (core * half, at * WIDE), (half, count * WIDE)) for w in (w_gate, w_up)], 1
        )

    first_sent = after(
        (gate_part(0, GROUPS[0]), lax.dynamic_slice(w_down, (core * (late // 2), 0), (late // 2, width))),
        in_blocks,
    )
    first = cross(first_sent)
    flat_in = after(proj_in, first_sent).reshape(width, 3 * channels)
    proj_out_far = far_join(out_half, 0)

    order = block_order(me, dp, width, bits)
    cot_t = ordered(order, after(cotangent, first_sent))

    resid_in = tokens.astype(jnp.float32)
    scale_mix = lax.rsqrt(jnp.mean(resid_in * resid_in, axis=-1, keepdims=True) + epsilon)
    unit_mix = resid_in * scale_mix
    normed = (unit_mix * gain_mix).astype(jnp.bfloat16)
    normed_t = ordered(order, after(normed, first_sent))
    kept = mixer_forward(after(normed, first_sent), flat_in, taps)
    kept_far = mixer_forward(normed, flat_in_far, taps_far)
    mixer = times_rows(kept[-1], proj_out) + times_rows(kept_far[-1], proj_out_far)
    middle = resid_in + mixer
    scale_ffn = lax.rsqrt(jnp.mean(middle * middle, axis=-1, keepdims=True) + epsilon)
    unit_ffn = middle * scale_ffn
    normed_mid = (unit_ffn * gain_ffn).astype(jnp.bfloat16)
    normed_mid_t = ordered(order, normed_mid)
    first = after(first, middle)
    rest = (hidden - late) // dp
    down_blocks = cross(lax.dynamic_slice_in_dim(after(w_down, first), late + me * rest, rest, 0))
    down_late = gathered(down_blocks)

    def gate_send(index, received):
        part = after(gate_part(sum(GROUPS[:index]), GROUPS[index]), received)
        return part, cross(part)

    parts = []
    received = first

    def far_part(index, gates_far, down_far, down_at, *others):
        sums, grads = ffn_part(
            after(normed_mid, others),
            normed_mid_t,
            cotangent,
            cot_t,
            gates_far,
            gates_far,
            down_far,
            0,
            GROUPS[index],
            down_at,
            GROUPS[index],
        )
        parts.append(sums)
        return grads

    def near_part(index, *others):
        at = sum(GROUPS[:index])
        sums, grads = ffn_part(
            after(normed_mid, others), normed_mid_t, cotangent, cot_t, w_gate, w_up, w_down, at, at, at, GROUPS[index]
        )
        parts.append(sums)
        return grads

    def chain(grads):
        return Chain(dp, [grads[0], swap(grads[1], dp, 0)])

    gates0, down0 = far_join(first[0], 0), far_join(first[1], 0)
    sending, second = gate_send(1, (first, down_blocks))
    grads = far_part(0, gates0, down0, 0, sending, cot_t, normed_t)
    far0 = chain(grads)
    sending, third = gate_send(2, second)
    grads = near_part(0, grads, sending)
    near0 = chain(grads)
    gates1 = far_join(second, 0)
    grads = far_part(1, gates1, down_late, 0, grads, far0.halve(grads))
    far1 = chain(grads)
    grads = near_part(1, grads, near0.halve(grads), far0.halve(grads))
    near1 = chain(grads)
    gates2 = far_join(after(third, grads), 0)
    grads = far_part(2, gates2, down_late, GROUPS[1], grads, near1.take(far1, grads), far0.halve(grads), near0.halve(grads))
    far2 = chain(grads)
    near1.terms = [add(*near1.terms[:2]), near1.terms[2]]
    far0.settle(grads)
    grads = near_part(2, grads, near0.halve(grads), near1.terms[0], far0.terms)
    near2 = chain(grads)
    branch = sum(part[0].astype(jnp.float32) for part in parts)
    grad_mid = sum(part[1].astype(jnp.float32) for part in parts)
    grad_mid = after(grad_mid, near0.take(far0, grads), near2.take(far2, grads))
    near2.terms = [after(add(*near2.terms[:2]), grad_mid), near2.terms[2]]
    grad_gain_ffn = jnp.sum(grad_mid * unit_ffn, axis=0)
    grad_middle = cotangent.astype(jnp.float32) + norm_back(grad_mid * gain_ffn, unit_ffn, scale_ffn)
    mixer_cot = grad_middle.astype(jnp.bfloat16)
    mixer_cot = after(mixer_cot, near1.halve(grad_mid), near2.terms[0])
    mixer_cot_t = ordered(order, mixer_cot)
    grad_taps, grad_proj = mixer_backward(right_outer(mixer_cot, proj_out), kept, taps)
    grad_taps_far, grad_proj_far = mixer_backward(right_outer(mixer_cot, proj_out_far), kept_far, taps_far)

    def mixer_grads(grad_proj, gated):
        return tuple(
            jnp.concatenate(
                [times_rows(normed_t[part], grad_proj), times_rows(mixer_cot_t[part], gated)], 1
            ).astype(jnp.bfloat16)
            for part in (slice(0, half), slice(half, width))
        )

    both = (grad_proj, grad_proj_far)
    both = after(both, near0.gather(both))
    grads = mixer_grads(both[1], kept_far[-1])
    far3 = chain(grads)
    grads = mixer_grads(after(both[0], grads), kept[-1])
    near3 = chain(grads)
    near4, token4 = near3.take_cut(far3, slice(0, 2 * channels), grads)
    near5, token5 = near3.take_cut(far3, slice(2 * channels, 4 * channels), grads)
    near4.terms = [add(*near4.terms[:2]), near4.terms[2]]
    near5.terms = [add(*near5.terms[:2]), near5.terms[2]]
    grad_proj, grad_proj_far = after(both, token4, token5, near4.terms[0], near5.terms[0])

    grad_normed = right_outer(grad_proj, flat_in) + right_outer(grad_proj_far, flat_in_far)
    grad_gain_mix = jnp.sum(grad_normed * unit_mix, axis=0)
    grad_tokens = grad_middle + norm_back(grad_normed * gain_mix, unit_mix, scale_mix)

    output = (middle + branch).astype(jnp.bfloat16)
    gains = jnp.concatenate([grad_gain_mix[None], grad_gain_ffn[None]], 0)
    small = jnp.concatenate([gains[:, :channels], gains[:, channels:], grad_taps, grad_taps_far], 0)
    for bit in (0,) + bits[2:] + (1,):
        small = small + swap(small, dp, bit)
    small = small[0:7] + cross(jnp.concatenate([small[0:4], small[7:10]], 0))
    gains = jnp.concatenate([small[0:2], small[2:4]], 1)
    orders = (order.T, order)
    token = near1.halve(grad_normed)
    token = near2.halve(token)
    token = near1.halve(token, grad_tokens, output)
    token = near4.halve(token)
    token = near2.halve(token)
    token = near1.gather(token, near0.result)
    token = near5.halve(token)
    token = near4.halve(token)
    token = near2.halve(token)
    token = near5.halve(token)
    token = near4.halve(token)
    token = near5.halve(token)
    token = near4.collect(token)
    totals = ffn_final(after(near0.result, token), None, 0, hidden, orders)
    token = near5.collect(token, totals[0])
    token = near2.gather(token, near1.result)
    totals = ffn_final(near1.result, totals, GROUPS[0], hidden, orders)
    token = (token, totals[0])
    for _ in bits[1:]:
        token = near4.collect(token)
        token = near5.collect(token)
    totals = ffn_final(near2.result, totals, sum(GROUPS[:2]), hidden, orders)
    grad_w_gate, grad_w_up, grad_w_down = totals
    grad_proj_in, grad_proj_out = mixer_final(near4.result, near5.result, orders)
    return (
        output,
        grad_tokens,
        gains[0],
        grad_proj_in.transpose(1, 0, 2),
        small[4:7],
        grad_proj_out,
        gains[1],
        grad_w_gate,
        grad_w_up,
        grad_w_down,
    )


def solution(mesh):
    placed = (
        P(("dp", "tensor"), None),
        P(),
        P(None, None, "tensor"),
        P(None, "tensor"),
        P("tensor", None),
        P(),
        P(None, "tensor"),
        P(None, "tensor"),
        P("tensor", None),
        P(("dp", "tensor"), None),
    )
    sizes = (mesh.shape["dp"], mesh.shape["tensor"])

    def block(*args):
        if fits(sizes, args):
            return paired_shards(sizes[0], *args)
        return split_shards(*args)

    return jax.shard_map(
        block,
        mesh=mesh,
        in_specs=placed,
        out_specs=(
            P(("dp", "tensor"), None),
            P(("dp", "tensor"), None),
            P(),
            P(None, None, "tensor"),
            P(None, "tensor"),
            P("tensor", None),
            P(),
            P(None, "tensor"),
            P(None, "tensor"),
            P("tensor", None),
        ),
        check_vma=False,
    )
```

```python
import functools

import jax
import jax.numpy as jnp
from jax import lax
from jax.experimental import pallas as pl
from jax.experimental.pallas import tpu as pltpu
from jax.sharding import PartitionSpec as P

LEN = 512


epsilon = 1e-05


def times_rows(left, right):
    return jnp.dot(left, right, preferred_element_type=jnp.float32)


def left_outer(left, right):
    return lax.dot_general(
        left, right, (((0,), (0,)), ((), ())), preferred_element_type=jnp.float32
    )


def right_outer(left, right):
    return lax.dot_general(
        left, right, (((1,), (1,)), ((), ())), preferred_element_type=jnp.float32
    )


def row_position(values):
    return lax.broadcasted_iota(jnp.int32, (values.shape[0], 1), 0) % LEN


def shift_down(values, steps):
    shifted = jnp.concatenate(
        [jnp.zeros((steps, values.shape[1]), values.dtype), values[:-steps]], 0
    )
    return jnp.where(row_position(values) >= steps, shifted, jnp.zeros_like(shifted))


def shift_up(values, steps):
    masked = jnp.where(row_position(values) >= steps, values, jnp.zeros_like(values))
    return jnp.concatenate([masked[steps:], jnp.zeros((steps, values.shape[1]), values.dtype)], 0)


def norm_back(grad_unit, unit, scale):
    return scale * (grad_unit - unit * jnp.mean(grad_unit * unit, axis=-1, keepdims=True))


def split_shards(
    tokens, gain_mix, proj_in, conv_filter, proj_out, gain_ffn, w_gate, w_up, w_down, cotangent
):
    model_width = tokens.shape[1]
    channels = proj_in.shape[2]
    resid_in = tokens.astype(jnp.float32)
    scale_mix = lax.rsqrt(jnp.mean(resid_in * resid_in, axis=-1, keepdims=True) + epsilon)
    unit_mix = resid_in * scale_mix
    normed = (unit_mix * gain_mix).astype(jnp.bfloat16)
    normed_all = lax.all_gather(normed, "tensor", axis=0, tiled=True)
    flat_in = proj_in.reshape(model_width, 3 * channels)
    projected = times_rows(normed_all, flat_in).reshape(-1, 3, channels)
    gate_b = projected[:, 0]
    gate_c = projected[:, 1]
    values = projected[:, 2]
    mixed_in = gate_b * values
    back_one = shift_down(mixed_in, 1)
    back_two = shift_down(mixed_in, 2)
    convolved = conv_filter[2] * mixed_in + conv_filter[1] * back_one + conv_filter[0] * back_two
    gated = (gate_c * convolved).astype(jnp.bfloat16)
    mixer = lax.psum_scatter(times_rows(gated, proj_out), "tensor", scatter_dimension=0, tiled=True)
    middle = resid_in + mixer
    scale_ffn = lax.rsqrt(jnp.mean(middle * middle, axis=-1, keepdims=True) + epsilon)
    unit_ffn = middle * scale_ffn
    normed_mid = (unit_ffn * gain_ffn).astype(jnp.bfloat16)
    grad_out = cotangent.astype(jnp.float32)
    mid_all = lax.all_gather(normed_mid, "tensor", axis=0, tiled=True)
    gate_value = times_rows(mid_all, w_gate)
    up_value = times_rows(mid_all, w_up)
    sigmoid_gate = jax.nn.sigmoid(gate_value)
    hidden = (gate_value * sigmoid_gate * up_value).astype(jnp.bfloat16)
    branch = lax.psum_scatter(times_rows(hidden, w_down), "tensor", scatter_dimension=0, tiled=True)
    cot_all = lax.all_gather(cotangent, "tensor", axis=0, tiled=True)
    grad_hidden = right_outer(cot_all, w_down)
    grad_gate = (
        grad_hidden * up_value * sigmoid_gate * (1.0 + gate_value * (1.0 - sigmoid_gate))
    ).astype(jnp.bfloat16)
    grad_upper = (grad_hidden * gate_value * sigmoid_gate).astype(jnp.bfloat16)
    grad_w_down = left_outer(hidden, cot_all)
    grad_w_gate = left_outer(mid_all, grad_gate)
    grad_w_up = left_outer(mid_all, grad_upper)
    grad_mid = lax.psum_scatter(
        right_outer(grad_gate, w_gate) + right_outer(grad_upper, w_up),
        "tensor",
        scatter_dimension=0,
        tiled=True,
    )
    output = (middle + branch).astype(jnp.bfloat16)
    grad_gain_ffn = jnp.sum(grad_mid * unit_ffn, axis=0)
    grad_middle = grad_out + norm_back(grad_mid * gain_ffn, unit_ffn, scale_ffn)
    mixer_cot = grad_middle.astype(jnp.bfloat16)
    cot_mix_all = lax.all_gather(mixer_cot, "tensor", axis=0, tiled=True)
    grad_proj_out = left_outer(gated, cot_mix_all)
    grad_gated = right_outer(cot_mix_all, proj_out)
    grad_cgate = grad_gated * convolved
    grad_conv = grad_gated * gate_c
    grad_conv_filter = jnp.stack(
        [
            jnp.sum(grad_conv * back_two, axis=0),
            jnp.sum(grad_conv * back_one, axis=0),
            jnp.sum(grad_conv * mixed_in, axis=0),
        ],
        0,
    )
    grad_mixed = (
        conv_filter[2] * grad_conv
        + conv_filter[1] * shift_up(grad_conv, 1)
        + conv_filter[0] * shift_up(grad_conv, 2)
    )
    grad_proj = (
        jnp.stack([grad_mixed * values, grad_cgate, grad_mixed * gate_b], 1)
        .astype(jnp.bfloat16)
        .reshape(-1, 3 * channels)
    )
    grad_proj_in = left_outer(normed_all, grad_proj).reshape(model_width, 3, channels)
    grad_normed = lax.psum_scatter(
        right_outer(grad_proj, flat_in), "tensor", scatter_dimension=0, tiled=True
    )
    grad_gain_mix = jnp.sum(grad_normed * unit_mix, axis=0)
    grad_tokens = grad_middle + norm_back(grad_normed * gain_mix, unit_mix, scale_mix)
    grad_gain_mix, grad_gain_ffn = lax.psum((grad_gain_mix, grad_gain_ffn), ("dp", "tensor"))
    grad_proj_in, grad_conv_filter, grad_proj_out, grad_w_gate, grad_w_up, grad_w_down = lax.psum(
        (grad_proj_in, grad_conv_filter, grad_proj_out, grad_w_gate, grad_w_up, grad_w_down), "dp"
    )
    return (
        output,
        grad_tokens,
        grad_gain_mix,
        grad_proj_in,
        grad_conv_filter,
        grad_proj_out,
        grad_gain_ffn,
        grad_w_gate,
        grad_w_up,
        grad_w_down,
    )


WIDE = 256
ROW_TILE = 512
GROUPS = (3, 3, 3)
MIB = 1024 * 1024


def fits(sizes, args):
    dp, tensor = sizes
    tokens, proj_in, w_gate = args[0], args[2], args[6]
    return (
        tensor == 2
        and dp & (dp - 1) == 0
        and 4 <= dp <= 16
        and tokens.shape[0] % LEN == 0
        and tokens.shape[1] == 1024
        and proj_in.shape[2] % 128 == 0
        and w_gate.shape[1] == WIDE * sum(GROUPS)
    )


def ffn_body(h, ht, e, et, wg, wu, wd, branch, grad_h, keep, send, zs, gg, gu, branch_sum, grad_sum):
    rows, half, wide = h.shape[0], keep.shape[0], wg.shape[1]
    step = pl.program_id(0)

    @pl.when(step == 0)
    def _():
        branch_sum[...] = jnp.zeros_like(branch_sum)
        grad_sum[...] = jnp.zeros_like(grad_sum)

    for start in range(0, rows, ROW_TILE):
        r = pl.ds(start, ROW_TILE)
        gate = times_rows(h[r, :], wg[...])
        up = times_rows(h[r, :], wu[...])
        grad_hidden = right_outer(e[r, :], wd[...])
        s = jax.nn.sigmoid(gate)
        gs = gate * s
        hidden = (gs * up).astype(jnp.bfloat16)
        grad_up = (grad_hidden * gs).astype(jnp.bfloat16)
        grad_gate = (grad_hidden * up * (s + gs * (1.0 - s))).astype(jnp.bfloat16)
        zs[r, :] = hidden
        gg[r, :] = grad_gate
        gu[r, :] = grad_up
        branch_sum[r, :] += times_rows(hidden, wd[...])
        grad_sum[r, :] += right_outer(grad_gate, wg[...]) + right_outer(grad_up, wu[...])
    for out, base in ((keep, 0), (send, half)):
        a = ht[pl.ds(base, half), :]
        out[:, 0:wide] = times_rows(a, gg[...]).astype(jnp.bfloat16)
        out[:, wide : 2 * wide] = times_rows(a, gu[...]).astype(jnp.bfloat16)
        out[:, 2 * wide : 3 * wide] = times_rows(et[pl.ds(base, half), :], zs[...]).astype(jnp.bfloat16)

    @pl.when(step == pl.num_programs(0) - 1)
    def _():
        branch[...] = branch_sum[...].astype(jnp.bfloat16)
        grad_h[...] = grad_sum[...].astype(jnp.bfloat16)


def ffn_part(h, ht, e, et, wg, wu, wd, gate_at, up_at, down_at, count):
    rows, width = h.shape

    def whole(shape):
        return pl.BlockSpec(shape, lambda j: (0, 0), pipeline_mode=pl.Buffered(1))

    branch, grad_h, keep, send = pl.pallas_call(
        ffn_body,
        grid=(count,),
        in_specs=[
            whole((rows, width)),
            whole((width, rows)),
            whole((rows, width)),
            whole((width, rows)),
            pl.BlockSpec((width, WIDE), lambda j: (0, gate_at + j)),
            pl.BlockSpec((width, WIDE), lambda j: (0, up_at + j)),
            pl.BlockSpec((WIDE, width), lambda j: (down_at + j, 0)),
        ],
        out_specs=[pl.BlockSpec((rows, width), lambda j: (0, 0))] * 2
        + [pl.BlockSpec((width // 2, 3 * WIDE), lambda j: (0, j))] * 2,
        out_shape=[jax.ShapeDtypeStruct((rows, width), jnp.bfloat16)] * 2
        + [jax.ShapeDtypeStruct((width // 2, 3 * WIDE * count), jnp.bfloat16)] * 2,
        scratch_shapes=[pltpu.VMEM((rows, WIDE), jnp.bfloat16)] * 3
        + [pltpu.VMEM((rows, width), jnp.float32)] * 2,
        compiler_params=pltpu.CompilerParams(vmem_limit_bytes=56 * MIB),
        cost_estimate=pl.CostEstimate(
            flops=8 * rows * width * WIDE * count, bytes_accessed=MIB, transcendentals=0
        ),
    )(h, ht, e, et, wg, wu, wd)
    return (branch, grad_h), (keep, send)


def ffn_final_body(restored, *refs):
    gate, up, down = refs[-3:]
    cuts = [slice(k * WIDE, (k + 1) * WIDE) for k in range(3)]
    if restored:
        grads = refs[0]
        gate[...] = grads[:, cuts[0]].astype(jnp.float32)
        up[...] = grads[:, cuts[1]].astype(jnp.float32)
        down[...] = grads[:, cuts[2]].astype(jnp.float32).T
        return
    own, other, restore, order = refs[:4]
    half = own.shape[0]
    gate[...] = times_rows(restore[:, :half], own[:, cuts[0]]) + times_rows(restore[:, half:], other[:, cuts[0]])
    up[...] = times_rows(restore[:, :half], own[:, cuts[1]]) + times_rows(restore[:, half:], other[:, cuts[1]])
    down[...] = left_outer(own[:, cuts[2]], order[:half, :]) + left_outer(other[:, cuts[2]], order[half:, :])


def ffn_final(grads, totals, at, columns, orders):
    restored = len(grads) == 1
    width = orders[0].shape[0]
    count = grads[0].shape[1] // (3 * WIDE)
    old = [] if totals is None else list(totals)
    new = list(grads) if restored else list(grads) + list(orders)
    return pl.pallas_call(
        functools.partial(ffn_final_body, restored),
        grid=(count,),
        in_specs=[pl.BlockSpec((g.shape[0], 3 * WIDE), lambda j: (0, j)) for g in grads]
        + [pl.BlockSpec(g.shape, lambda j: (0, 0)) for g in new[len(grads) :]]
        + [pl.BlockSpec(memory_space=pl.ANY)] * len(old),
        out_specs=[
            pl.BlockSpec((width, WIDE), lambda j: (0, at + j)),
            pl.BlockSpec((width, WIDE), lambda j: (0, at + j)),
            pl.BlockSpec((WIDE, width), lambda j: (at + j, 0)),
        ],
        out_shape=[
            jax.ShapeDtypeStruct((width, columns), jnp.float32),
            jax.ShapeDtypeStruct((width, columns), jnp.float32),
            jax.ShapeDtypeStruct((columns, width), jnp.float32),
        ],
        input_output_aliases={len(new) + i: i for i in range(len(old))},
        compiler_params=pltpu.CompilerParams(vmem_limit_bytes=40 * MIB),
        cost_estimate=pl.CostEstimate(flops=MIB, bytes_accessed=MIB, transcendentals=0),
    )(*new, *old)


def swap(values, dp, bit):
    return lax.ppermute(values, "dp", [(i, i ^ (1 << bit)) for i in range(dp)])


def cross(values):
    return jax.tree.map(lambda v: lax.ppermute(v, "tensor", [(0, 1), (1, 0)]), values)


def add(*terms):
    total = terms[0].astype(jnp.float32)
    for term in terms[1:]:
        total = total + term.astype(jnp.float32)
    return total.astype(terms[0].dtype)


def after(values, *others):
    return lax.optimization_barrier((values, others))[0]


class Chain:
    def __init__(self, dp, terms, bit=0):
        self.dp, self.bit, self.terms = dp, bit, terms

    def halve(self, *others):
        terms = after(self.terms, *others)
        half = terms[0].shape[0] // 2
        total = add(*[t[half:] for t in terms])
        self.bit += 1
        self.terms = [add(*[t[:half] for t in terms]), swap(total, self.dp, self.bit)]
        return total

    def total(self):
        return add(*self.terms)

    def settle(self, *others):
        total = after(self.total(), *others)
        self.terms = [total]
        return total

    def take(self, other, *others):
        total = after(other.total(), *others)
        self.terms = self.terms + [cross(total)]
        return total

    def take_cut(self, other, cut, *others):
        total = after(add(*[t[:, cut] for t in other.terms]), *others)
        part = Chain(self.dp, [t[:, cut] for t in self.terms] + [cross(total)], self.bit)
        return part, total

    def gather(self, *others):
        total = after(self.total(), *others)
        self.result = (lax.all_gather(total, "dp", axis=0, tiled=True),)
        return total

    def collect(self, *others):
        total = after(jnp.concatenate(self.terms, 0) if self.bit < 0 else self.total(), *others)
        self.bit = ~self.bit if self.bit >= 0 else self.bit
        self.terms = [total, swap(total, self.dp, ~self.bit)]
        self.bit += 1
        self.result = tuple(self.terms)
        return total


def mixer_final_body(own1, other1, own2, other2, restore, order, grad_in, grad_out):
    channels = grad_in.shape[2]
    half = own1.shape[0]
    low, high = restore[:, :half], restore[:, half:]
    for k, (own, other, at) in enumerate(((own1, other1, 0), (own1, other1, 1), (own2, other2, 0))):
        cut = slice(at * channels, (at + 1) * channels)
        grad_in[k] = times_rows(low, own[:, cut]) + times_rows(high, other[:, cut])
    cut = slice(channels, 2 * channels)
    grad_out[...] = left_outer(own2[:, cut], order[:half, :]) + left_outer(other2[:, cut], order[half:, :])


def mixer_final(first, second, orders):
    half, pair = first[0].shape
    width, channels, rows = 2 * half, pair // 2, 256
    return pl.pallas_call(
        mixer_final_body,
        grid=(width // rows,),
        in_specs=[pl.BlockSpec((half, pair), lambda j: (0, 0))] * 4
        + [pl.BlockSpec((rows, width), lambda j: (j, 0)), pl.BlockSpec((width, rows), lambda j: (0, j))],
        out_specs=[
            pl.BlockSpec((3, rows, channels), lambda j: (0, j, 0)),
            pl.BlockSpec((channels, rows), lambda j: (0, j)),
        ],
        out_shape=[
            jax.ShapeDtypeStruct((3, width, channels), jnp.float32),
            jax.ShapeDtypeStruct((channels, width), jnp.float32),
        ],
        compiler_params=pltpu.CompilerParams(vmem_limit_bytes=40 * MIB),
        cost_estimate=pl.CostEstimate(flops=MIB, bytes_accessed=MIB, transcendentals=0),
    )(*first, *second, *orders)


def block_order(me, dp, width, bits):
    rows = lax.broadcasted_iota(jnp.int32, (width, width), 0)
    columns = lax.broadcasted_iota(jnp.int32, (width, width), 1)
    size = width // dp
    block = rows // size
    owner = jnp.zeros_like(block)
    for place, bit in enumerate(reversed(bits)):
        owner = owner | (((block >> place) & 1) << bit)
    return (columns == (owner ^ me) * size + rows % size).astype(jnp.bfloat16)


def ordered(order, values):
    return right_outer(order, values).astype(jnp.bfloat16)


def mixer_forward(normed, flat_in, taps):
    channels = taps.shape[1]
    projected = times_rows(normed, flat_in)
    gate_b = projected[:, :channels]
    gate_c = projected[:, channels : 2 * channels]
    values = projected[:, 2 * channels :]
    mixed_in = gate_b * values
    back_one = shift_down(mixed_in, 1)
    back_two = shift_down(mixed_in, 2)
    convolved = taps[2] * mixed_in + taps[1] * back_one + taps[0] * back_two
    gated = (gate_c * convolved).astype(jnp.bfloat16)
    return gate_b, gate_c, values, mixed_in, back_one, back_two, convolved, gated


def mixer_backward(grad_gated, kept, taps):
    gate_b, gate_c, values, mixed_in, back_one, back_two, convolved, _ = kept
    grad_cgate = grad_gated * convolved
    grad_conv = grad_gated * gate_c
    grad_taps = jnp.stack(
        [
            jnp.sum(grad_conv * back_two, axis=0),
            jnp.sum(grad_conv * back_one, axis=0),
            jnp.sum(grad_conv * mixed_in, axis=0),
        ],
        0,
    )
    grad_mixed = taps[2] * grad_conv + taps[1] * shift_up(grad_conv, 1) + taps[0] * shift_up(grad_conv, 2)
    grad_proj = jnp.concatenate(
        [grad_mixed * values, grad_cgate, grad_mixed * gate_b], 1
    ).astype(jnp.bfloat16)
    return grad_taps, grad_proj


def paired_shards(
    dp, tokens, gain_mix, proj_in, taps, proj_out, gain_ffn, w_gate, w_up, w_down, cotangent
):
    me = lax.axis_index("dp")
    core = me & 1
    width = tokens.shape[1]
    channels = proj_in.shape[2]
    hidden = w_gate.shape[1]
    bits = tuple(range(dp.bit_length() - 1))

    def gathered(blocks):
        return lax.all_gather(blocks, "dp", axis=0, tiled=True)

    half = width // 2
    def my_rows(values):
        size = values.shape[0] // dp
        return lax.dynamic_slice_in_dim(values, me * size, size, 0)

    in_blocks = cross(my_rows(proj_in).reshape(width // dp, 3 * channels))
    out_half = cross(lax.dynamic_slice_in_dim(proj_out, core * (channels // 2), channels // 2, 0))
    taps_far = cross(taps)
    flat_in_far = gathered(in_blocks)
    late = GROUPS[0] * WIDE

    def far_join(mine, axis):
        other = swap(mine, dp, 0)
        return jnp.concatenate([jnp.where(core == 0, mine, other), jnp.where(core == 0, other, mine)], axis)

    def gate_part(at, count):
        return jnp.concatenate(
            [lax.dynamic_slice(w, (core * half, at * WIDE), (half, count * WIDE)) for w in (w_gate, w_up)], 1
        )

    first_sent = after(
        (gate_part(0, GROUPS[0]), lax.dynamic_slice(w_down, (core * (late // 2), 0), (late // 2, width))),
        in_blocks,
    )
    first = cross(first_sent)
    flat_in = after(proj_in, first_sent).reshape(width, 3 * channels)
    proj_out_far = far_join(out_half, 0)

    order = block_order(me, dp, width, bits)
    cot_t = ordered(order, after(cotangent, first_sent))

    resid_in = tokens.astype(jnp.float32)
    scale_mix = lax.rsqrt(jnp.mean(resid_in * resid_in, axis=-1, keepdims=True) + epsilon)
    unit_mix = resid_in * scale_mix
    normed = (unit_mix * gain_mix).astype(jnp.bfloat16)
    normed_t = ordered(order, after(normed, first_sent))
    kept = mixer_forward(after(normed, first_sent), flat_in, taps)
    kept_far = mixer_forward(normed, flat_in_far, taps_far)
    mixer = times_rows(kept[-1], proj_out) + times_rows(kept_far[-1], proj_out_far)
    middle = resid_in + mixer
    scale_ffn = lax.rsqrt(jnp.mean(middle * middle, axis=-1, keepdims=True) + epsilon)
    unit_ffn = middle * scale_ffn
    normed_mid = (unit_ffn * gain_ffn).astype(jnp.bfloat16)
    normed_mid_t = ordered(order, normed_mid)
    first = after(first, middle)
    rest = (hidden - late) // dp
    down_blocks = cross(lax.dynamic_slice_in_dim(after(w_down, first), late + me * rest, rest, 0))
    down_late = gathered(down_blocks)

    def gate_send(index, received):
        part = after(gate_part(sum(GROUPS[:index]), GROUPS[index]), received)
        return part, cross(part)

    parts = []
    received = first

    def far_part(index, gates_far, down_far, down_at, *others):
        sums, grads = ffn_part(
            after(normed_mid, others),
            normed_mid_t,
            cotangent,
            cot_t,
            gates_far,
            gates_far,
            down_far,
            0,
            GROUPS[index],
            down_at,
            GROUPS[index],
        )
        parts.append(sums)
        return grads

    def near_part(index, *others):
        at = sum(GROUPS[:index])
        sums, grads = ffn_part(
            after(normed_mid, others), normed_mid_t, cotangent, cot_t, w_gate, w_up, w_down, at, at, at, GROUPS[index]
        )
        parts.append(sums)
        return grads

    def chain(grads):
        return Chain(dp, [grads[0], swap(grads[1], dp, 0)])

    gates0, down0 = far_join(first[0], 0), far_join(first[1], 0)
    sending, second = gate_send(1, (first, down_blocks))
    grads = far_part(0, gates0, down0, 0, sending, cot_t, normed_t)
    far0 = chain(grads)
    sending, third = gate_send(2, second)
    grads = near_part(0, grads, sending)
    near0 = chain(grads)
    gates1 = far_join(second, 0)
    grads = far_part(1, gates1, down_late, 0, grads, far0.halve(grads))
    far1 = chain(grads)
    grads = near_part(1, grads, near0.halve(grads), far0.halve(grads))
    near1 = chain(grads)
    gates2 = far_join(after(third, grads), 0)
    grads = far_part(2, gates2, down_late, GROUPS[1], grads, near1.take(far1, grads), far0.halve(grads), near0.halve(grads))
    far2 = chain(grads)
    near1.terms = [add(*near1.terms[:2]), near1.terms[2]]
    far0.settle(grads)
    grads = near_part(2, grads, near0.halve(grads), near1.terms[0], far0.terms)
    near2 = chain(grads)
    branch = sum(part[0].astype(jnp.float32) for part in parts)
    grad_mid = sum(part[1].astype(jnp.float32) for part in parts)
    grad_mid = after(grad_mid, near0.take(far0, grads), near2.take(far2, grads))
    near2.terms = [after(add(*near2.terms[:2]), grad_mid), near2.terms[2]]
    grad_gain_ffn = jnp.sum(grad_mid * unit_ffn, axis=0)
    grad_middle = cotangent.astype(jnp.float32) + norm_back(grad_mid * gain_ffn, unit_ffn, scale_ffn)
    mixer_cot = grad_middle.astype(jnp.bfloat16)
    mixer_cot = after(mixer_cot, near1.halve(grad_mid), near2.terms[0])
    mixer_cot_t = ordered(order, mixer_cot)
    grad_taps, grad_proj = mixer_backward(right_outer(mixer_cot, proj_out), kept, taps)
    grad_taps_far, grad_proj_far = mixer_backward(right_outer(mixer_cot, proj_out_far), kept_far, taps_far)

    def mixer_grads(grad_proj, gated):
        return tuple(
            jnp.concatenate(
                [times_rows(normed_t[part], grad_proj), times_rows(mixer_cot_t[part], gated)], 1
            ).astype(jnp.bfloat16)
            for part in (slice(0, half), slice(half, width))
        )

    both = (grad_proj, grad_proj_far)
    both = after(both, near0.gather(both))
    grads = mixer_grads(both[1], kept_far[-1])
    far3 = chain(grads)
    grads = mixer_grads(after(both[0], grads), kept[-1])
    near3 = chain(grads)
    near4, token4 = near3.take_cut(far3, slice(0, 2 * channels), grads)
    near5, token5 = near3.take_cut(far3, slice(2 * channels, 4 * channels), grads)
    near4.terms = [add(*near4.terms[:2]), near4.terms[2]]
    near5.terms = [add(*near5.terms[:2]), near5.terms[2]]
    grad_proj, grad_proj_far = after(both, token4, token5, near4.terms[0], near5.terms[0])

    grad_normed = right_outer(grad_proj, flat_in) + right_outer(grad_proj_far, flat_in_far)
    grad_gain_mix = jnp.sum(grad_normed * unit_mix, axis=0)
    grad_tokens = grad_middle + norm_back(grad_normed * gain_mix, unit_mix, scale_mix)

    output = (middle + branch).astype(jnp.bfloat16)
    gains = jnp.concatenate([grad_gain_mix[None], grad_gain_ffn[None]], 0)
    small = jnp.concatenate([gains[:, :channels], gains[:, channels:], grad_taps, grad_taps_far], 0)
    for bit in (0,) + bits[2:] + (1,):
        small = small + swap(small, dp, bit)
    small = small[0:7] + cross(jnp.concatenate([small[0:4], small[7:10]], 0))
    gains = jnp.concatenate([small[0:2], small[2:4]], 1)
    orders = (order.T, order)
    token = near1.halve(grad_normed)
    token = near2.halve(token)
    token = near1.halve(token, grad_tokens, output)
    token = near4.halve(token)
    token = near2.halve(token)
    token = near1.gather(token, near0.result)
    token = near5.halve(token)
    token = near4.halve(token)
    token = near2.halve(token)
    token = near5.halve(token)
    token = near4.halve(token)
    token = near5.halve(token)
    token = near4.collect(token)
    totals = ffn_final(after(near0.result, token), None, 0, hidden, orders)
    token = near5.collect(token, totals[0])
    token = near2.gather(token, near1.result)
    totals = ffn_final(near1.result, totals, GROUPS[0], hidden, orders)
    token = (token, totals[0])
    for _ in bits[1:]:
        token = near4.collect(token)
        token = near5.collect(token)
    totals = ffn_final(near2.result, totals, sum(GROUPS[:2]), hidden, orders)
    grad_w_gate, grad_w_up, grad_w_down = totals
    grad_proj_in, grad_proj_out = mixer_final(near4.result, near5.result, orders)
    return (
        output,
        grad_tokens,
        gains[0],
        grad_proj_in.transpose(1, 0, 2),
        small[4:7],
        grad_proj_out,
        gains[1],
        grad_w_gate,
        grad_w_up,
        grad_w_down,
    )


def solution(mesh):
    placed = (
        P(("dp", "tensor"), None),
        P(),
        P(None, None, "tensor"),
        P(None, "tensor"),
        P("tensor", None),
        P(),
        P(None, "tensor"),
        P(None, "tensor"),
        P("tensor", None),
        P(("dp", "tensor"), None),
    )
    sizes = (mesh.shape["dp"], mesh.shape["tensor"])

    def block(*args):
        if fits(sizes, args):
            return paired_shards(sizes[0], *args)
        return split_shards(*args)

    return jax.shard_map(
        block,
        mesh=mesh,
        in_specs=placed,
        out_specs=(
            P(("dp", "tensor"), None),
            P(("dp", "tensor"), None),
            P(),
            P(None, None, "tensor"),
            P(None, "tensor"),
            P("tensor", None),
            P(),
            P(None, "tensor"),
            P(None, "tensor"),
            P("tensor", None),
        ),
        check_vma=False,
    )
```
